32 devices in a mesh: dp: 8 (over z, core), vocab: 4 (over y, x).
Axes of the slice: x: 2, y: 2, z: 4, core: 2. Of those that a mesh axis runs over, the one named last changes fastest.
Arguments:
- hidden: bfloat16 [2048, 4096], P('dp')
- table: bfloat16 [16384, 4096], P(('vocab', 'dp')), as said below
- targets: int32 [2048], P('dp'), may hold values from 0 to 16383
- token_scale: float32 [2048], P('dp'), may hold values from 2 to 32
- enc_ids: int32 [512], P(('dp', 'vocab')), may hold values from 0 to 16383
- enc_cot: bfloat16 [512, 4096], P(('dp', 'vocab')), may hold values from -6 to 6
- dec_ids: int32 [512], P(('dp', 'vocab')), may hold values from 0 to 16383
- dec_cot: bfloat16 [512, 4096], P(('dp', 'vocab')), may hold values from -6 to 6
Outputs:
- grad_hidden: bfloat16 [2048, 4096], P('dp', 'vocab')
- grad_table: float32 [16384, 4096], P(('vocab', 'dp'))
- loss: float32 [2048], P('dp')
The draws below stay inside these ranges and needn't reach their ends.
Inputs may be any that keep to these rules, and one draw needn't show every extreme that they name: table entries of order 3 / sqrt(4096).
All inputs are finite; a program needn't handle non-finite values.
Results may differ from the reference program's by a relative error of at most 0.018.
Values may be sent and summed in bfloat16 or wider, within the bound.
A program may use at most 192 MiB of HBM per device.

```python
import math
import jax
import jax.numpy as jnp
import numpy as np
from jax import lax

D = 4096
V = 16384
TOK_DEV = 256
IDS_DEV = 16
TOKENS = 2048
IDS = 512
N_DP = 8
N_VOCAB = 4


def shared_table(key):
    noise = jax.random.normal(jax.random.fold_in(key, 11), (V, D), jnp.float32)
    return jnp.clip(noise, -4.0, 4.0) * (3.0 / D ** 0.5)


def draw_table(key, part):
    return shared_table(key).astype(jnp.bfloat16)


def draw_hidden(key, part):
    return jax.random.normal(jax.random.fold_in(key, 12), (TOKENS, D), jnp.float32).astype(jnp.bfloat16)


def plant(values, stream_key, low, high):
    dims = values.shape
    spot = [jax.random.randint(jax.random.fold_in(stream_key, axis), (), 0, dims[axis]) for axis in range(len(dims))]
    values = values.at[tuple(spot)].set(low)
    longest = dims.index(max(dims))
    spot[longest] = (spot[longest] + 1) % dims[longest]
    return values.at[tuple(spot)].set(high)


def level_of(stream_key, extent, shards, least, top_value):
    factor_of, own = 1.0, jax.random.fold_in(stream_key, 6)
    for position, shards_of in shards:
        heights = jnp.exp(jax.random.uniform(jax.random.fold_in(own, position), (shards_of,), jnp.float32, least / len(shards), top_value / len(shards)))
        factor_of = factor_of * jnp.repeat(heights, extent[position] // shards_of).reshape([-1 if axis == position else 1 for axis in range(len(extent))])
    return factor_of


def cumulative_ranks(amount, lean):
    portions = [(1 << 20) // math.isqrt(standing ** lean) + 1 for standing in range(1, amount + 1)]
    deviation = 1 + sum(portions) // (1 << 30)
    return np.cumsum(np.array([max(1, weight // deviation) for weight in portions]))


def ranked(key, dims, amount, skew):
    table = cumulative_ranks(amount, skew)
    pick = jax.random.randint(jax.random.fold_in(key, 1), dims, 0, int(table[amount - 1]))
    standing = jnp.searchsorted(jnp.asarray(table, jnp.int32), pick, side="right")
    return jax.random.permutation(jax.random.fold_in(key, 2), amount)[standing].astype(jnp.int32)


def bell_draw(stream_key, dims, width, most, cuts=(), kind=jnp.bfloat16):
    values = jax.random.normal(stream_key, dims, jnp.float32) * width
    if len(cuts) > 0:
        values = level_of(stream_key, dims, cuts, -0.22, 0.18) * values
    return jnp.clip(values, min=-most, max=most).astype(kind)


def setup_inputs(seed: int = 0) -> dict:
    keys = jax.random.split(jax.random.key(seed), 9)
    hidden = draw_hidden(jax.random.fold_in(keys[8], 71), 0)
    table = draw_table(jax.random.fold_in(keys[8], 71), 0)
    targets = plant(ranked(keys[2], (TOKENS,), V, 2), jax.random.fold_in(keys[2], 3), 0, V - 1).astype(jnp.int32)
    token_scale = jnp.clip(jnp.exp(math.log(32.0) - 2.7725887 * jax.random.uniform(keys[3], (TOKENS,), jnp.float32) ** level_of(keys[3], (TOKENS,), ((0, 8),), -0.2, 0.2)), 2.0, 32.0)
    enc_ids = plant(ranked(keys[4], (IDS,), V, 2), jax.random.fold_in(keys[4], 3), 0, V - 1).astype(jnp.int32)
    enc_cot = bell_draw(keys[5], (IDS, D), 1.0, 6.0, ((0, 32),))
    dec_ids = plant(ranked(keys[6], (IDS,), V, 3), jax.random.fold_in(keys[6], 3), 0, V - 1).astype(jnp.int32)
    dec_cot = bell_draw(keys[7], (IDS, D), 1.0, 6.0, ((0, 32),))
    return {"hidden": hidden, "table": table, "targets": targets, "token_scale": token_scale, "enc_ids": enc_ids, "enc_cot": enc_cot, "dec_ids": dec_ids, "dec_cot": dec_cot}


def reference(hidden, table, targets, token_scale, enc_ids, enc_cot, dec_ids, dec_cot):
    group_ids = IDS_DEV * N_VOCAB

    def one_group(total, index):
        rows = (index * TOK_DEV).astype(jnp.int32)
        id_start = (index * group_ids).astype(jnp.int32)
        states = lax.dynamic_slice_in_dim(hidden, rows, TOK_DEV, 0)
        wanted = lax.dynamic_slice_in_dim(targets, rows, TOK_DEV, 0)
        scales = lax.dynamic_slice_in_dim(token_scale, rows, TOK_DEV, 0)
        logits = jnp.dot(states, table.T, preferred_element_type=jnp.float32)
        row_max = jnp.max(logits, axis=1)
        expo = jnp.exp(logits - row_max[:, None])
        row_sum = jnp.sum(expo, axis=1)
        target_logit = jnp.take_along_axis(logits, wanted[:, None], axis=1)[:, 0]
        loss = row_max + jnp.log(row_sum) - target_logit
        matches = (jnp.arange(V, dtype=jnp.int32)[None, :] == wanted[:, None]).astype(jnp.float32)
        dlogits = (scales[:, None] * (expo / row_sum[:, None] - matches)).astype(jnp.bfloat16)
        grad_states = jnp.dot(dlogits, table, preferred_element_type=jnp.float32).astype(jnp.bfloat16)
        head = jnp.dot(dlogits.T, states, preferred_element_type=jnp.float32)
        ids_one = lax.dynamic_slice_in_dim(enc_ids, id_start, group_ids, 0)
        cot_one = lax.dynamic_slice_in_dim(enc_cot, id_start, group_ids, 0).astype(jnp.float32)
        ids_two = lax.dynamic_slice_in_dim(dec_ids, id_start, group_ids, 0)
        cot_two = lax.dynamic_slice_in_dim(dec_cot, id_start, group_ids, 0).astype(jnp.float32)
        head = head.at[ids_one].add(cot_one).at[ids_two].add(cot_two)
        rounded = lax.optimization_barrier(head.astype(jnp.bfloat16))
        return total + rounded.astype(jnp.float32), (grad_states, loss)

    start = jnp.zeros((V, D), jnp.float32)
    total, (grad_parts, loss_parts) = lax.scan(one_group, start, jnp.arange(N_DP, dtype=jnp.int32))
    grad_hidden = grad_parts.reshape(TOKENS, D)
    loss = loss_parts.reshape(TOKENS)
    return grad_hidden, total, loss
```

```python
import jax
import jax.numpy as jnp
from jax import lax
from jax.sharding import PartitionSpec as P

F32 = jnp.float32
BOTH = ("dp", "vocab")


def dot(a, b, dims):
    return lax.dot_general(a, b, (dims, ((), ())), preferred_element_type=F32)


def shards(hidden, table, targets, token_scale, enc_ids, enc_cot, dec_ids, dec_cot):
    n_dp, n_vocab = lax.axis_size("dp"), lax.axis_size("vocab")
    me_dp, me_vocab = lax.axis_index("dp"), lax.axis_index("vocab")
    tok, width = hidden.shape
    rows = table.shape[0]
    cols = width // n_vocab
    tokens = tok * n_dp
    offset = (me_vocab * n_dp + me_dp) * rows

    mine = lax.dynamic_slice_in_dim(hidden, me_vocab * cols, cols, 1)
    states = lax.all_gather(mine, BOTH, axis=0).reshape(n_dp, n_vocab, tok, cols)
    states = [states[:, v].reshape(tokens, cols) for v in range(n_vocab)]
    parts = [table[:, v * cols:(v + 1) * cols] for v in range(n_vocab)]

    small = lax.all_gather(
        jnp.stack([targets.astype(F32), token_scale]), "dp", axis=0
    )
    all_targets = small[:, 0].reshape(tokens).astype(jnp.int32) - offset
    all_scale = small[:, 1].reshape(tokens)

    logits = sum(dot(h, t, ((1,), (1,))) for h, t in zip(states, parts))
    columns = jnp.arange(rows, dtype=jnp.int32)
    matches = columns[None, :] == all_targets[:, None]
    target_part = jnp.sum(jnp.where(matches, logits, 0.0), axis=1)
    local_max = jnp.max(logits, axis=1)
    local_sum = jnp.sum(jnp.exp(logits - local_max[:, None]), axis=1)
    stats = lax.all_gather(jnp.stack([local_max, local_sum, target_part]), BOTH, axis=0)
    row_max = jnp.max(stats[:, 0], axis=0)
    row_sum = jnp.sum(stats[:, 1] * jnp.exp(stats[:, 0] - row_max[None]), axis=0)
    target_logit = jnp.sum(stats[:, 2], axis=0)
    loss = row_max + jnp.log(row_sum) - target_logit
    loss = lax.dynamic_slice_in_dim(loss, me_dp * tok, tok, 0)

    dlogits = (
        all_scale[:, None]
        * (jnp.exp(logits - row_max[:, None]) / row_sum[:, None] - matches.astype(F32))
    ).astype(jnp.bfloat16)

    everyone = n_dp * n_vocab
    steps = 1 if tokens * width * 2 <= (16 << 20) else 4
    short = tok // steps
    by_group = dlogits.reshape(n_dp, tok, rows)
    done = []
    for step in range(steps):
        part = by_group[:, step * short:(step + 1) * short].reshape(n_dp * short, rows)
        if done:
            part, done[-1] = lax.optimization_barrier((part, done[-1]))
        terms = [
            dot(part, t, ((1,), (0,))).astype(jnp.bfloat16).reshape(n_dp, short, cols)
            for t in parts
        ]
        terms = jnp.stack(terms, axis=1).reshape(everyone, short, cols)
        done.append(lax.psum_scatter(terms, BOTH, scatter_dimension=0, tiled=False))
    grad_hidden = jnp.concatenate(done, axis=0)

    head = jnp.concatenate([dot(dlogits, h, ((0,), (0,))) for h in states], axis=1)

    ids = jnp.concatenate([enc_ids, dec_ids])
    cots = jnp.concatenate([enc_cot, dec_cot], axis=0)
    per = ids.shape[0]
    pieces = max(1, everyone * per * width * 2 // (8 << 20))
    all_ids = lax.all_gather(ids.reshape(pieces, per // pieces), BOTH, axis=1, tiled=True)

    def add(total, piece):
        one_ids, one_cots = piece
        got = lax.all_gather(one_cots, BOTH, axis=0, tiled=True)
        hits = (columns[:, None] == (one_ids - offset)[None, :]).astype(jnp.bfloat16)
        return total + dot(hits, got, ((1,), (0,))), None

    cots = cots.reshape(pieces, per // pieces, width)
    if pieces == 1:
        grad_table, _ = add(head, (all_ids[0], cots[0]))
    else:
        grad_hidden, head = lax.optimization_barrier((grad_hidden, head))
        grad_table, _ = lax.scan(add, head, (all_ids, cots))
    return (grad_hidden, grad_table, loss)


def solution(mesh):
    placed = (
        P("dp", None),
        P(("vocab", "dp"), None),
        P("dp"),
        P("dp"),
        P(("dp", "vocab")),
        P(("dp", "vocab"), None),
        P(("dp", "vocab")),
        P(("dp", "vocab"), None),
    )
    return jax.shard_map(
        shards,
        mesh=mesh,
        in_specs=placed,
        out_specs=(P("dp", "vocab"), P(("vocab", "dp"), None), P("dp")),
        check_vma=False,
    )
```

```python
import jax
import jax.numpy as jnp
from jax import lax
from jax.sharding import PartitionSpec as P

F32 = jnp.float32
BOTH = ("dp", "vocab")


def dot(a, b, dims):
    return lax.dot_general(a, b, (dims, ((), ())), preferred_element_type=F32)


def plus(kept, got):
    return (kept.astype(F32) + got.astype(F32)).astype(jnp.bfloat16)


def scatter_by_axes(dlogits, table, tok):
    n_dp, me_dp = lax.axis_size("dp"), lax.axis_index("dp")
    me_vocab = lax.axis_index("vocab")
    n_z = n_dp // 2
    z, core, y, x = me_dp // 2, me_dp % 2, me_vocab // 2, me_vocab % 2
    rows, width = table.shape
    cols = width // 4

    groups = dlogits.reshape(n_z, 2, tok, rows)

    def term(which):
        part = lax.dynamic_index_in_dim(groups, which, 1, keepdims=False)
        return dot(part.reshape(n_z * tok, rows), table, ((1,), (0,)))

    twin = [(i, i ^ 1) for i in range(n_dp)]
    got = lax.ppermute(term(1 - core).astype(jnp.bfloat16), "dp", twin)
    both = plus(term(core), got).reshape(n_z, tok, width)

    along_x = [(v, v ^ 1) for v in range(4)]
    along_y = [(v, v ^ 2) for v in range(4)]

    def block(array, index, many=1):
        return lax.dynamic_slice_in_dim(array, index * cols, many * cols, 2)

    def pair(array, index):
        return jnp.concatenate([block(array, index), block(array, 2 + index)], axis=2)

    one, two = both[:, :tok // 2], both[:, tok // 2:]
    got_one = lax.ppermute(pair(one, 1 - x), "vocab", along_x)
    got_two = lax.ppermute(block(two, 2 * (1 - y), 2), "vocab", along_y)
    one = plus(pair(one, x), got_one)
    two = plus(block(two, 2 * y, 2), got_two)
    got_one = lax.ppermute(block(one, 1 - y), "vocab", along_y)
    got_two = lax.ppermute(block(two, 1 - x), "vocab", along_x)
    one = plus(block(one, y), got_one)
    two = plus(block(two, x), got_two)
    mine = jnp.concatenate([one, two], axis=1)

    total = lax.dynamic_index_in_dim(mine, z, 0, keepdims=False).astype(F32)
    for shift in range(1, n_z):
        sent = lax.dynamic_index_in_dim(mine, (z + shift) % n_z, 0, keepdims=False)
        hop = [(i, (i + 2 * shift) % n_dp) for i in range(n_dp)]
        total = total + lax.ppermute(sent, "dp", hop).astype(F32)
    return total.astype(jnp.bfloat16)


def scatter_whole(dlogits, parts, tok):
    n_dp, everyone = lax.axis_size("dp"), lax.axis_size(BOTH)
    rows, cols = parts[0].shape
    steps = 4
    short = tok // steps
    by_group = dlogits.reshape(n_dp, tok, rows)
    done = []
    for step in range(steps):
        part = by_group[:, step * short:(step + 1) * short].reshape(n_dp * short, rows)
        if done:
            part, done[-1] = lax.optimization_barrier((part, done[-1]))
        terms = [
            dot(part, t, ((1,), (0,))).astype(jnp.bfloat16).reshape(n_dp, short, cols)
            for t in parts
        ]
        terms = jnp.stack(terms, axis=1).reshape(everyone, short, cols)
        done.append(lax.psum_scatter(terms, BOTH, scatter_dimension=0, tiled=False))
    return jnp.concatenate(done, axis=0)


def shards(hidden, table, targets, token_scale, enc_ids, enc_cot, dec_ids, dec_cot):
    n_dp, n_vocab = lax.axis_size("dp"), lax.axis_size("vocab")
    me_dp, me_vocab = lax.axis_index("dp"), lax.axis_index("vocab")
    tok, width = hidden.shape
    rows = table.shape[0]
    cols = width // n_vocab
    tokens = tok * n_dp
    offset = (me_vocab * n_dp + me_dp) * rows

    mine = lax.dynamic_slice_in_dim(hidden, me_vocab * cols, cols, 1)
    states = lax.all_gather(mine, BOTH, axis=0).reshape(n_dp, n_vocab, tok, cols)
    states = [states[:, v].reshape(tokens, cols) for v in range(n_vocab)]
    parts = [table[:, v * cols:(v + 1) * cols] for v in range(n_vocab)]

    small = lax.all_gather(
        jnp.stack([targets.astype(F32), token_scale]), "dp", axis=0
    )
    all_targets = small[:, 0].reshape(tokens).astype(jnp.int32) - offset
    all_scale = small[:, 1].reshape(tokens)

    logits = sum(dot(h, t, ((1,), (1,))) for h, t in zip(states, parts))
    columns = jnp.arange(rows, dtype=jnp.int32)
    matches = columns[None, :] == all_targets[:, None]
    target_part = jnp.sum(jnp.where(matches, logits, 0.0), axis=1)
    local_max = jnp.max(logits, axis=1)
    local_sum = jnp.sum(jnp.exp(logits - local_max[:, None]), axis=1)
    ids = jnp.concatenate([enc_ids, dec_ids])
    per = ids.shape[0]
    cots = jnp.concatenate([enc_cot, dec_cot], axis=0)
    own = jnp.concatenate([local_max, local_sum, target_part, ids.astype(F32)])
    own = jnp.pad(own, (0, -own.shape[0] % 1024)).reshape(-1, 128)
    stats = lax.all_gather(own, BOTH, axis=0).reshape(n_dp * n_vocab, -1)
    stats, cots = lax.optimization_barrier((stats, cots))
    id_rows = stats[:, 3 * tokens:3 * tokens + per].astype(jnp.int32)
    stats = stats[:, :3 * tokens].reshape(-1, 3, tokens)
    row_max = jnp.max(stats[:, 0], axis=0)
    row_sum = jnp.sum(stats[:, 1] * jnp.exp(stats[:, 0] - row_max[None]), axis=0)
    target_logit = jnp.sum(stats[:, 2], axis=0)
    loss = row_max + jnp.log(row_sum) - target_logit
    loss = lax.dynamic_slice_in_dim(loss, me_dp * tok, tok, 0)

    dlogits = (
        all_scale[:, None]
        * (jnp.exp(logits - row_max[:, None]) / row_sum[:, None] - matches.astype(F32))
    ).astype(jnp.bfloat16)

    everyone = n_dp * n_vocab
    if n_vocab == 4 and n_dp % 2 == 0:
        grad_hidden = scatter_by_axes(dlogits, table, tok)
    else:
        grad_hidden = scatter_whole(dlogits, parts, tok)

    head = jnp.concatenate([dot(dlogits, h, ((0,), (0,))) for h in states], axis=1)

    pieces = max(1, everyone * per * width * 2 // (8 << 20))
    all_ids = id_rows.reshape(everyone, pieces, per // pieces)
    all_ids = all_ids.swapaxes(0, 1).reshape(pieces, everyone * (per // pieces))

    def add(total, piece):
        one_ids, one_cots = piece
        got = lax.all_gather(one_cots, BOTH, axis=0, tiled=True)
        hits = (columns[:, None] == (one_ids - offset)[None, :]).astype(jnp.bfloat16)
        return total + dot(hits, got, ((1,), (0,))), None

    cots = cots.reshape(pieces, per // pieces, width)
    if pieces == 1:
        grad_table, _ = add(head, (all_ids[0], cots[0]))
    else:
        grad_hidden, head = lax.optimization_barrier((grad_hidden, head))
        grad_table, _ = lax.scan(add, head, (all_ids, cots))
    return (grad_hidden, grad_table, loss)


def solution(mesh):
    placed = (
        P("dp", None),
        P(("vocab", "dp"), None),
        P("dp"),
        P("dp"),
        P(("dp", "vocab")),
        P(("dp", "vocab"), None),
        P(("dp", "vocab")),
        P(("dp", "vocab"), None),
    )
    return jax.shard_map(
        shards,
        mesh=mesh,
        in_specs=placed,
        out_specs=(P("dp", "vocab"), P(("vocab", "dp"), None), P("dp")),
        check_vma=False,
    )
```

```python
import jax
import jax.numpy as jnp
from jax import lax
from jax.sharding import PartitionSpec as P

F32 = jnp.float32
BOTH = ("dp", "vocab")


def dot(a, b, dims):
    return lax.dot_general(a, b, (dims, ((), ())), preferred_element_type=F32)


def plus(kept, got):
    return (kept.astype(F32) + got.astype(F32)).astype(jnp.bfloat16)


def scatter_by_axes(dlogits, table, tok):
    n_dp, me_dp = lax.axis_size("dp"), lax.axis_index("dp")
    me_vocab = lax.axis_index("vocab")
    n_z = n_dp // 2
    z, core, y, x = me_dp // 2, me_dp % 2, me_vocab // 2, me_vocab % 2
    rows, width = table.shape
    cols = width // 4

    groups = dlogits.reshape(n_z, 2, tok, rows)

    def term(which):
        part = lax.dynamic_index_in_dim(groups, which, 1, keepdims=False)
        return dot(part.reshape(n_z * tok, rows), table, ((1,), (0,)))

    twin = [(i, i ^ 1) for i in range(n_dp)]
    got = lax.ppermute(term(1 - core).astype(jnp.bfloat16), "dp", twin)
    both = plus(term(core), got).reshape(n_z, tok, width)

    along_x = [(v, v ^ 1) for v in range(4)]
    along_y = [(v, v ^ 2) for v in range(4)]

    def block(array, index, many=1):
        return lax.dynamic_slice_in_dim(array, index * cols, many * cols, 2)

    def pair(array, index):
        return jnp.concatenate([block(array, index), block(array, 2 + index)], axis=2)

    one, two = both[:, :tok // 2], both[:, tok // 2:]
    got_one = lax.ppermute(pair(one, 1 - x), "vocab", along_x)
    got_two = lax.ppermute(block(two, 2 * (1 - y), 2), "vocab", along_y)
    one = plus(pair(one, x), got_one)
    two = plus(block(two, 2 * y, 2), got_two)
    got_one = lax.ppermute(block(one, 1 - y), "vocab", along_y)
    got_two = lax.ppermute(block(two, 1 - x), "vocab", along_x)
    one = plus(block(one, y), got_one)
    two = plus(block(two, x), got_two)
    mine = jnp.concatenate([one, two], axis=1)

    total = lax.dynamic_index_in_dim(mine, z, 0, keepdims=False).astype(F32)
    for shift in range(1, n_z):
        sent = lax.dynamic_index_in_dim(mine, (z + shift) % n_z, 0, keepdims=False)
        hop = [(i, (i + 2 * shift) % n_dp) for i in range(n_dp)]
        total = total + lax.ppermute(sent, "dp", hop).astype(F32)
    return total.astype(jnp.bfloat16)


def scatter_whole(dlogits, parts, tok):
    n_dp, everyone = lax.axis_size("dp"), lax.axis_size(BOTH)
    rows, cols = parts[0].shape
    steps = 4
    short = tok // steps
    by_group = dlogits.reshape(n_dp, tok, rows)
    done = []
    for step in range(steps):
        part = by_group[:, step * short:(step + 1) * short].reshape(n_dp * short, rows)
        if done:
            part, done[-1] = lax.optimization_barrier((part, done[-1]))
        terms = [
            dot(part, t, ((1,), (0,))).astype(jnp.bfloat16).reshape(n_dp, short, cols)
            for t in parts
        ]
        terms = jnp.stack(terms, axis=1).reshape(everyone, short, cols)
        done.append(lax.psum_scatter(terms, BOTH, scatter_dimension=0, tiled=False))
    return jnp.concatenate(done, axis=0)


def shards(hidden, table, targets, token_scale, enc_ids, enc_cot, dec_ids, dec_cot):
    n_dp, n_vocab = lax.axis_size("dp"), lax.axis_size("vocab")
    me_dp, me_vocab = lax.axis_index("dp"), lax.axis_index("vocab")
    tok, width = hidden.shape
    rows = table.shape[0]
    cols = width // n_vocab
    tokens = tok * n_dp
    offset = (me_vocab * n_dp + me_dp) * rows

    mine = lax.dynamic_slice_in_dim(hidden, me_vocab * cols, cols, 1)
    states = lax.all_gather(mine, BOTH, axis=0).reshape(n_dp, n_vocab, tok, cols)
    states = [states[:, v].reshape(tokens, cols) for v in range(n_vocab)]
    parts = [table[:, v * cols:(v + 1) * cols] for v in range(n_vocab)]

    small = lax.all_gather(
        jnp.stack([targets.astype(F32), token_scale]), "dp", axis=0
    )
    all_targets = small[:, 0].reshape(tokens).astype(jnp.int32) - offset
    all_scale = small[:, 1].reshape(tokens)

    logits = sum(dot(h, t, ((1,), (1,))) for h, t in zip(states, parts))
    columns = jnp.arange(rows, dtype=jnp.int32)
    matches = columns[None, :] == all_targets[:, None]
    target_part = jnp.sum(jnp.where(matches, logits, 0.0), axis=1)
    local_max = jnp.max(logits, axis=1)
    local_sum = jnp.sum(jnp.exp(logits - local_max[:, None]), axis=1)
    ids = jnp.concatenate([enc_ids, dec_ids])
    per = ids.shape[0]
    cots = jnp.concatenate([enc_cot, dec_cot], axis=0)
    merged = (local_max, local_sum, target_part)
    id_rows = ids.astype(F32)[None]
    for axis in ("vocab", "dp"):
        own = jnp.concatenate([*merged, id_rows.reshape(-1)])
        size = own.shape[0]
        own = jnp.pad(own, (0, -size % 1024)).reshape(-1, 128)
        stats = lax.all_gather(own, axis, axis=0).reshape(lax.axis_size(axis), -1)
        id_rows = stats[:, 3 * tokens:size]
        stats = stats[:, :3 * tokens].reshape(-1, 3, tokens)
        row_max = jnp.max(stats[:, 0], axis=0)
        row_sum = jnp.sum(stats[:, 1] * jnp.exp(stats[:, 0] - row_max[None]), axis=0)
        target_logit = jnp.sum(stats[:, 2], axis=0)
        merged = (row_max, row_sum, target_logit)
    row_max, cots = lax.optimization_barrier((row_max, cots))
    id_rows = id_rows.astype(jnp.int32)
    loss = row_max + jnp.log(row_sum) - target_logit
    loss = lax.dynamic_slice_in_dim(loss, me_dp * tok, tok, 0)

    dlogits = (
        all_scale[:, None]
        * (jnp.exp(logits - row_max[:, None]) / row_sum[:, None] - matches.astype(F32))
    ).astype(jnp.bfloat16)

    everyone = n_dp * n_vocab
    if n_vocab == 4 and n_dp % 2 == 0:
        grad_hidden = scatter_by_axes(dlogits, table, tok)
    else:
        grad_hidden = scatter_whole(dlogits, parts, tok)

    head = jnp.concatenate([dot(dlogits, h, ((0,), (0,))) for h in states], axis=1)

    pieces = max(1, everyone * per * width * 2 // (8 << 20))
    all_ids = id_rows.reshape(everyone, pieces, per // pieces)
    all_ids = all_ids.swapaxes(0, 1).reshape(pieces, everyone * (per // pieces))

    def add(total, piece):
        one_ids, one_cots = piece
        got = lax.all_gather(one_cots, BOTH, axis=0, tiled=True)
        hits = (columns[:, None] == (one_ids - offset)[None, :]).astype(jnp.bfloat16)
        return total + dot(hits, got, ((1,), (0,))), None

    cots = cots.reshape(pieces, per // pieces, width)
    if pieces == 1:
        grad_table, _ = add(head, (all_ids[0], cots[0]))
    else:
        grad_hidden, head = lax.optimization_barrier((grad_hidden, head))
        grad_table, _ = lax.scan(add, head, (all_ids, cots))
    return (grad_hidden, grad_table, loss)


def solution(mesh):
    placed = (
        P("dp", None),
        P(("vocab", "dp"), None),
        P("dp"),
        P("dp"),
        P(("dp", "vocab")),
        P(("dp", "vocab"), None),
        P(("dp", "vocab")),
        P(("dp", "vocab"), None),
    )
    return jax.shard_map(
        shards,
        mesh=mesh,
        in_specs=placed,
        out_specs=(P("dp", "vocab"), P(("vocab", "dp"), None), P("dp")),
        check_vma=False,
    )
```
